256 devices in a mesh: dom: 128 (over x, y, z), rep: 2 (over core).
Axes of the slice: x: 4, y: 4, z: 8, core: 2. Of those that a mesh axis runs over, the one named last changes fastest.
Arguments:
- features: bfloat16 [131072, 256], P(('dom', 'rep')), may hold values from -6 to 6
- w_self: bfloat16 [256, 256], replicated, may hold values from -0.375 to 0.375
- w_neigh: bfloat16 [256, 256], replicated, may hold values from -0.375 to 0.375
- bias_vector: float32 [256], replicated, may hold values from -3 to 3
- upstream: bfloat16 [131072, 256], P(('dom', 'rep')), may hold values from -6 to 6
- sources: int32 [1048576], P(('dom', 'rep')), may hold values from 0 to 1023
- edge_slots: int32 [1048576], P(('dom', 'rep')), may hold values from 0 to 2047, as said below
- mirror_rows: int32 [128, 128, 16], P('dom'), may hold values from 0 to 1023, as said below
Outputs:
- hidden: bfloat16 [131072, 256], P(('dom', 'rep'))
- input_grad: bfloat16 [131072, 256], P(('dom', 'rep'))
- grad_self: float32 [256, 256], replicated
- grad_neigh: float32 [256, 256], replicated
- grad_bias: float32 [256], replicated
The draws below stay inside these ranges and needn't reach their ends.
Inputs may be any that keep to these rules, and one draw needn't show every extreme that they name: `edge_slots`: slot s stands for column s % 16 of partition s // 16. mirror_rows[q, p, c] is a master row of partition q; the 16 rows of one [q, p] are different.
All inputs are finite; a program needn't handle non-finite values.
Results may differ from the reference program's by a relative error of at most 0.007.
Values may be sent and summed in bfloat16 or wider, within the bound.
A program may use at most 64 MiB of HBM per device.

```python
import math
import jax
import jax.numpy as jnp
import numpy as np
from jax import lax

F = 256
H = 256
E_DEV = 4096
CAP = 16
PARTITIONS = 128
HELPERS = 2
V_PART = 1024
VERTS = 131072
EDGES = 1048576


def draw_edge_slots(key, part):
    key = jax.random.fold_in(key, 11)
    key_spread, key_part, key_hub, key_choose = jax.random.split(key, 4)
    edge_shape = (EDGES,)
    spread_slot = jax.random.randint(key_spread, edge_shape, 0, PARTITIONS * CAP)
    target_part = jax.random.randint(key_part, edge_shape, 0, PARTITIONS)
    hub_slot = target_part * CAP + jax.random.randint(key_hub, edge_shape, 0, CAP // 4)
    choose_hub = jax.random.randint(key_choose, edge_shape, 0, 2)
    return jnp.where(choose_hub == 0, spread_slot, hub_slot).astype(jnp.int32)


def draw_mirror_rows(key, part):
    key = jax.random.fold_in(key, 23)
    key_hub, key_rest = jax.random.split(key, 2)
    hub_count = V_PART // 16
    hub_slots = CAP // 4
    hub_start = jax.random.randint(key_hub, (PARTITIONS, PARTITIONS, 1), 0, hub_count)
    rest_start = jax.random.randint(key_rest, (PARTITIONS, PARTITIONS, 1), 0, V_PART - hub_count)
    column = jnp.arange(CAP, dtype=jnp.int32)[None, None, :]
    hub_rows = (hub_start + column) % hub_count
    rest_rows = hub_count + (rest_start + column - hub_slots) % (V_PART - hub_count)
    return jnp.where(column < hub_slots, hub_rows, rest_rows).astype(jnp.int32)


def plant(result, key, smallest, largest):
    spot = [jax.random.randint(jax.random.fold_in(key, axis), (), 0, length) for axis, length in enumerate(result.shape)]
    main_axis = result.shape.index(max(result.shape))
    beside = spot[:main_axis] + [(spot[main_axis] + 1) % result.shape[main_axis]] + spot[main_axis + 1:]
    return result.at[tuple(spot)].set(smallest).at[tuple(beside)].set(largest)


def block_levels(stream_key, shape, pieces, least, top_value):
    factor_of = 1.0
    for position, parts in pieces:
        steps = jax.random.uniform(jax.random.fold_in(jax.random.fold_in(stream_key, 6), position), (parts,), jnp.float32, least / len(pieces), top_value / len(pieces))
        factor_of = factor_of * jnp.repeat(jnp.exp(steps), shape[position] // parts).reshape((-1,) + (1,) * (len(shape) - 1 - position))
    return factor_of


def rank_bounds(count, skew):
    weights = [(1 << 20) // math.isqrt(rank ** skew) + 1 for rank in range(1, count + 1)]
    width = 1 + sum(weights) // (1 << 30)
    return np.cumsum(np.array([max(1, weight // width) for weight in weights]))


def ranked_ids(own_key, shape, count, skew):
    listing = rank_bounds(count, skew)
    lot = jax.random.randint(jax.random.fold_in(own_key, 1), shape, 0, int(listing[count - 1]))
    standing = jnp.searchsorted(jnp.asarray(listing, jnp.int32), lot, side="right")
    return jax.random.permutation(jax.random.fold_in(own_key, 2), count)[standing].astype(jnp.int32)


def scatter_about(rng, extent, spread, bound, cuts=(), kind=jnp.bfloat16):
    values = spread * jax.random.normal(rng, extent, jnp.float32)
    if cuts:
        values = values * block_levels(rng, extent, cuts, -0.22, 0.18)
    return jnp.clip(values, -bound, bound).astype(kind)


def setup_inputs(seed: int = 0) -> dict:
    seeds = jax.random.split(jax.random.key(seed), 9)
    return {
        "features": scatter_about(seeds[0], (VERTS, F), 1.0, 6.0, ((0, 256),)),
        "w_self": scatter_about(seeds[1], (F, H), F ** -0.5, 0.375),
        "w_neigh": scatter_about(seeds[2], (F, H), F ** -0.5, 0.375),
        "bias_vector": scatter_about(seeds[3], (H,), 0.5, 3.0, (), jnp.float32),
        "upstream": scatter_about(seeds[4], (VERTS, H), 1.0, 6.0, ((0, 256),)),
        "sources": plant(ranked_ids(seeds[5], (EDGES,), V_PART, 2), jax.random.fold_in(seeds[5], 3), 0, V_PART - 1).astype(jnp.int32),
        "edge_slots": draw_edge_slots(jax.random.fold_in(seeds[8], 71), 0),
        "mirror_rows": draw_mirror_rows(jax.random.fold_in(seeds[8], 71), 0),
    }


def edge_targets(mirror_rows, partition, slot_row):
    target_table = jnp.arange(PARTITIONS, dtype=jnp.int32)[:, None] * V_PART + lax.dynamic_index_in_dim(mirror_rows, partition, 1, keepdims=False)
    return target_table.reshape(-1)[slot_row]

def reference(features, w_self, w_neigh, bias_vector, upstream, sources, edge_slots, mirror_rows):
    device_ids = jnp.arange(PARTITIONS * HELPERS, dtype=jnp.int32)
    source_rows = sources.reshape(PARTITIONS * HELPERS, E_DEV)
    slot_rows = edge_slots.reshape(PARTITIONS * HELPERS, E_DEV)

    def forward_step(running, inputs):
        summed, degree = running
        device, src_row, slot_row = inputs
        partition = device // HELPERS
        target = edge_targets(mirror_rows, partition, slot_row)
        source = partition * V_PART + src_row
        summed = summed.at[target].add(features[source].astype(jnp.float32))
        degree = degree.at[target].add(jnp.ones((E_DEV,), jnp.float32))
        return ((summed, degree), None)
    start = (jnp.zeros((VERTS, F), jnp.float32), jnp.zeros((VERTS,), jnp.float32))
    (neigh_sum, degree), _ = lax.scan(forward_step, start, (device_ids, source_rows, slot_rows))
    divisor = jnp.maximum(degree, 1.0)[:, None]
    neigh_mean = (neigh_sum / divisor).astype(jnp.bfloat16)
    pre = jnp.dot(features, w_self, preferred_element_type=jnp.float32) + jnp.dot(neigh_mean, w_neigh, preferred_element_type=jnp.float32) + bias_vector
    sigma = jax.nn.sigmoid(pre)
    hidden = (pre * sigma).astype(jnp.bfloat16)
    pre_grad = (upstream.astype(jnp.float32) * (sigma + pre * sigma * (1.0 - sigma))).astype(jnp.bfloat16)
    grad_scale = 1.0 / math.sqrt(VERTS)
    dims = (((0,), (0,)), ((), ()))
    grad_self = lax.dot_general(features, pre_grad, dims, preferred_element_type=jnp.float32) * grad_scale
    grad_neigh = lax.dot_general(neigh_mean, pre_grad, dims, preferred_element_type=jnp.float32) * grad_scale
    grad_bias = lax.optimization_barrier(jnp.sum(pre_grad.astype(jnp.float32), axis=0)) * grad_scale
    mean_grad = (jnp.dot(pre_grad, w_neigh.T, preferred_element_type=jnp.float32) / divisor).astype(jnp.bfloat16)
    self_grad = jnp.dot(pre_grad, w_self.T, preferred_element_type=jnp.float32)

    def backward_step(running, inputs):
        device, src_row, slot_row = inputs
        partition = device // HELPERS
        target = edge_targets(mirror_rows, partition, slot_row)
        source = partition * V_PART + src_row
        return (running.at[source].add(mean_grad[target].astype(jnp.float32)), None)
    edge_grad, _ = lax.scan(backward_step, jnp.zeros((VERTS, F), jnp.float32), (device_ids, source_rows, slot_rows))
    input_grad = (self_grad + edge_grad).astype(jnp.bfloat16)
    return (hidden, input_grad, grad_self, grad_neigh, grad_bias)
```

```python
import functools
import math

import jax
import jax.numpy as jnp
from jax import lax
from jax.experimental import pallas as pl
from jax.experimental.pallas import tpu as pltpu
from jax.sharding import PartitionSpec as P

MESH = pl.DeviceIdType.MESH
BF = jnp.bfloat16
F32 = jnp.float32
F8 = jnp.float8_e4m3fn

NN = (((1,), (0,)), ((), ()))
NT = (((1,), (1,)), ((), ()))
TN = (((0,), (0,)), ((), ()))

CHUNK = 2048
BLOCK = 256
MSG = 16


def dot(a, b, dims=NN):
    return lax.dot_general(a, b, dims, preferred_element_type=F32)


def one_hot_cols(index_row, count, dtype):
    n = index_row.shape[1]
    rows = lax.broadcasted_iota(jnp.int32, (count, n), 0).astype(jnp.int16)
    wanted = jnp.broadcast_to(index_row, (count, n)).astype(jnp.int16)
    return jnp.where(rows == wanted, jnp.ones((), BF), jnp.zeros((), BF)).astype(dtype)


def rows_at(start, count, unit):
    return pl.ds(pl.multiple_of(start, unit), count)


def kernel(
    feat, w_self, w_neigh, bias, up, src, slot, mir,
    hidden, igrad, gself, gneigh, gbias,
    psrc, pslot, fall, ssrc, at, sums, cnt, recv_f, crecv,
    pt, pm, nsum, nrecv, dpart, drecv, mg, gsend, recv_b, esum, erecv, selfg,
    term, trecv, rs, zr, ag, bb, bz, b2,
    rep_send, rep_recv, fs_sem, fr_sem, cs_sem, cr_sem, bs_sem, br_sem,
    ar_send, ar_recv,
):
    p = lax.axis_index("dom")
    r = lax.axis_index("rep")
    o = 1 - r
    x, y, z = p // 32, (p // 8) % 4, p % 8
    h, a, b = x // 2, x % 2, y // 2
    m = x * 4 + y
    my_idx = (a * 4 + y) * 8 + z
    is_home = h == r

    bar = pltpu.get_barrier_semaphore()

    def tell(dom, rep):
        pl.semaphore_signal(bar, inc=1, device_id=(dom, rep), device_id_type=MESH)

    tell(p, o)

    def tell_half(k, c):
        @pl.when(jnp.logical_not(jnp.logical_and(is_home, k == my_idx)))
        def _():
            tell(r * 64 + k, h)

        return c

    lax.fori_loop(0, 64, tell_half, 0)
    lax.fori_loop(1, 16, lambda k, c: (tell(((m + k) % 16) * 8 + z, r), c)[1], 0)
    lax.fori_loop(1, 8, lambda k, c: (tell(m * 8 + (z + k) % 8, r), c)[1], 0)

    own_rows = rows_at(r * 512, 512, 512)
    other_rows = rows_at(o * 512, 512, 512)

    for c in range(2):
        ssrc[c] = one_hot_cols(src[:, c * CHUNK:(c + 1) * CHUNK], 1024, F8)
    fall[own_rows, :] = feat[...]

    pl.semaphore_wait(bar, 87 - jnp.where(is_home, 1, 0))

    def to_other(source, target, n):
        return pltpu.make_async_remote_copy(
            source, target, rep_send.at[n], rep_recv.at[n],
            device_id=(p, o), device_id_type=MESH,
        )

    c_src = to_other(src, psrc, 0)
    c_slot = to_other(slot, pslot, 1)
    c_feat = to_other(feat, fall.at[own_rows, :], 2)
    c_src.start()
    c_slot.start()
    c_feat.start()
    c_src.wait_recv()
    for c in range(2):
        ssrc[2 + c] = one_hot_cols(psrc[:, c * CHUNK:(c + 1) * CHUNK], 1024, F8)
    c_slot.wait_recv()

    def send_block(t, source, target, send_sem, recv_sem, counts):
        i, j = (a + t // 2) % 2, (b + t % 2) % 2

        def step(k, c):
            line = i * 4 + 2 * j + k // 8
            idx = line * 8 + (z + k) % 8
            here = rows_at(idx * MSG, MSG, MSG)
            there = rows_at(my_idx * MSG, MSG, MSG)
            is_self = jnp.logical_and(is_home, idx == my_idx)

            @pl.when(jnp.logical_not(is_self))
            def _():
                dev = (r * 64 + idx, h)
                if counts:
                    pltpu.make_async_remote_copy(
                        cnt.at[line], crecv.at[my_idx], cs_sem, cr_sem,
                        device_id=dev, device_id_type=MESH,
                    ).start()
                pltpu.make_async_remote_copy(
                    source.at[here, :], target.at[there, :], send_sem, recv_sem.at[t],
                    device_id=dev, device_id_type=MESH,
                ).start()

            @pl.when(is_self)
            def _():
                if counts:
                    pltpu.make_async_copy(cnt.at[line], crecv.at[my_idx], cr_sem).start()
                pltpu.make_async_copy(source.at[here, :], target.at[there, :], recv_sem.at[t]).start()

            return c

        lax.fori_loop(0, 16, step, 0)

    def block_of(t):
        return (a + t // 2) % 2 * 2 + (b + t % 2) % 2

    def wait_block(t, target, recv_sem):
        part = target.at[rows_at(block_of(t) * BLOCK, BLOCK, BLOCK), :]
        pltpu.make_async_copy(part, part, recv_sem.at[t]).wait()

    for t in range(4):
        blk = block_of(t)
        base = r * 1024 + blk * BLOCK
        acc = None
        for c in range(4):
            row = slot if c < 2 else pslot
            lo = (c % 2) * CHUNK
            sel = one_hot_cols(row[:, lo:lo + CHUNK] - base, BLOCK, F8)
            d = dot(ssrc[c], sel, NT)
            acc = d if acc is None else acc + d
        counted = jnp.sum(acc, axis=0, keepdims=True)
        cnt[blk * 2] = counted[:, :128]
        cnt[blk * 2 + 1] = counted[:, 128:]
        table = acc.astype(BF)
        at[blk] = table
        if t == 0:
            c_feat.wait_recv()
        sums[rows_at(blk * BLOCK, BLOCK, BLOCK), :] = dot(table, fall[...], TN).astype(BF)
        send_block(t, sums, recv_f, fs_sem, fr_sem, True)

    mirror = mir[rows_at(r * 64, 64, 64), :]
    spread = jnp.broadcast_to(mirror[:, None, :], (64, 16, 16)).reshape(1024, 16)
    lane = lax.broadcasted_iota(jnp.int32, (1024, 16), 1)
    sub = lax.broadcasted_iota(jnp.int32, (1024, 16), 0)
    col = jnp.sum(jnp.where(lane == sub % 16, spread, 0), axis=1, keepdims=True)
    for q in range(4):
        part = col[q * BLOCK:(q + 1) * BLOCK]
        hit = lax.broadcasted_iota(jnp.int32, (BLOCK, 1024), 1) == part
        pt[q] = jnp.where(hit, 1.0, 0.0).astype(BF)
        row = jnp.broadcast_to(part.astype(F32), (BLOCK, 128)).T[0:1].astype(jnp.int32)
        pm[q] = one_hot_cols(row, 1024, BF)

    pre_self = dot(feat[...], w_self[...]) + bias[...]

    pltpu.make_async_copy(crecv, crecv, cr_sem).wait()
    got = crecv[...].reshape(64, 128)
    wide = jnp.broadcast_to(got[:, None, :], (64, 16, 128)).reshape(1024, 128)
    lane = lax.broadcasted_iota(jnp.int32, (1024, 128), 1)
    sub = lax.broadcasted_iota(jnp.int32, (1024, 128), 0)
    wide = jnp.where(lane == z * 16 + sub % 16, wide, 0.0)
    high = jnp.floor(wide * (1.0 / 256))
    split = jnp.concatenate([high, wide - high * 256.0], axis=1).astype(BF)
    both = sum(dot(pm[q], split[q * BLOCK:(q + 1) * BLOCK]) for q in range(4))
    dpart[...] = both[:, :128] * 256.0 + both[:, 128:]
    c_deg = to_other(dpart.at[other_rows, :], drecv, 3)
    c_deg.start()

    for t in range(4):
        blk = block_of(t)
        wait_block(t, recv_f, fr_sem)
        part = recv_f[rows_at(blk * BLOCK, BLOCK, BLOCK), :]
        if t == 0:
            nsum[...] = dot(pm[blk], part)
        elif t < 3:
            nsum[...] += dot(pm[blk], part)
        else:
            nsum[other_rows, :] += dot(pm[blk, other_rows, :], part)
            c_sum = to_other(nsum.at[other_rows, :], nrecv, 4)
            c_sum.start()
            mine = nsum[own_rows, :] + dot(pm[blk, own_rows, :], part)

    c_deg.wait_recv()
    degree = jnp.sum(dpart[own_rows, :] + drecv[...], axis=1, keepdims=True)
    divisor = jnp.maximum(degree, 1.0)
    c_sum.wait_recv()
    mean = ((mine + nrecv[...]) / divisor).astype(BF)
    pre = pre_self + dot(mean, w_neigh[...])
    gate = jax.nn.sigmoid(pre)
    pre_grad = (up[...].astype(F32) * (gate + pre * gate * (1.0 - gate))).astype(BF)
    mg[own_rows, :] = (dot(pre_grad, w_neigh[...], NT) / divisor).astype(BF)
    c_mg = to_other(mg.at[own_rows, :], mg.at[own_rows, :], 5)
    c_mg.start()
    term[0] = dot(feat[...], pre_grad, TN)
    term[1] = dot(mean, pre_grad, TN)
    c_term = to_other(term.at[o], trecv, 6)
    c_term.start()
    bb[m] = jnp.sum(pre_grad.astype(F32), axis=0, keepdims=True)

    def return_block(t):
        blk = block_of(t)
        here = rows_at(blk * BLOCK, BLOCK, BLOCK)
        gsend[here, :] = dot(pt[blk], mg[...]).astype(BF)
        send_block(t, gsend, recv_b, bs_sem, br_sem, False)

    def spread_to(peers, of, source, target, n):
        def step(k, c):
            pltpu.make_async_remote_copy(
                source(k), target, ar_send.at[n], ar_recv.at[n],
                device_id=(of(k), r), device_id_type=MESH,
            ).start()
            return c

        lax.fori_loop(1, peers, step, 0)

    def plane(k):
        return ((m + k) % 16) * 8 + z

    def line(k):
        return m * 8 + (z + k) % 8

    def wait_all(ref, count, sem):
        part = ref.at[pl.ds(0, count)]
        pltpu.make_async_copy(part, part, sem).wait()

    c_mg.wait_recv()
    return_block(0)
    hidden[...] = (pre * gate).astype(BF)
    selfg[...] = dot(pre_grad, w_self[...], NT)

    c_term.wait_recv()
    tsum = term.at[r]
    tsum[...] += trecv[...]
    spread_to(
        16, plane,
        lambda k: tsum.at[rows_at(((m + k) % 16) * 16, 16, 16), :], rs.at[m], 0,
    )
    spread_to(16, plane, lambda k: bb.at[m], bb.at[m], 1)
    rs[m] = tsum[rows_at(m * 16, 16, 16), :]
    return_block(1)

    wait_all(rs, 15, ar_recv.at[0])
    wait_all(bb, 15, ar_recv.at[1])
    zr[z] = jnp.sum(rs[...], axis=0)
    bz[z] = jnp.sum(bb[...], axis=0)
    spread_to(8, line, lambda k: zr.at[z], zr.at[z], 2)
    spread_to(8, line, lambda k: bz.at[z], bz.at[z], 3)
    return_block(2)

    scale = 1.0 / math.sqrt(131072)
    wait_all(zr, 7, ar_recv.at[2])
    wait_all(bz, 7, ar_recv.at[3])
    ag[r, m] = jnp.sum(zr[...], axis=0) * scale
    b2[r] = jnp.sum(bz[...], axis=0)
    spread_to(16, plane, lambda k: ag.at[r, m], ag.at[r, m], 4)
    c_bias = to_other(b2.at[r], b2.at[r], 7)
    c_bias.start()
    return_block(3)

    wait_all(ag.at[r], 15, ar_recv.at[4])
    c_ag = to_other(ag.at[r], ag.at[r], 8)
    c_ag.start()

    for t in range(4):
        blk = block_of(t)
        wait_block(t, recv_b, br_sem)
        part = recv_b[rows_at(blk * BLOCK, BLOCK, BLOCK), :]
        if t == 0:
            esum[...] = dot(at[blk], part)
        elif t < 3:
            esum[...] += dot(at[blk], part)
        else:
            esum[other_rows, :] += dot(at[blk, other_rows, :], part)
            c_edge = to_other(esum.at[other_rows, :], erecv, 9)
            c_edge.start()
            selfg[...] += esum[own_rows, :] + dot(at[blk, own_rows, :], part)

    c_bias.wait_recv()
    c_ag.wait_recv()
    gself[...] = ag[0].reshape(256, 256)
    gneigh[...] = ag[1].reshape(256, 256)
    gbias[...] = (b2[0] + b2[1]) * scale
    c_edge.wait_recv()
    igrad[...] = (selfg[...] + erecv[...]).astype(BF)

    for copy in (c_src, c_slot, c_feat, c_deg, c_sum, c_mg, c_term, c_bias, c_ag, c_edge):
        copy.wait_send()

    def sent(ref, count, sem):
        part = ref.at[pl.ds(0, count)]
        pltpu.make_async_copy(part, part, sem).wait()

    @pl.when(is_home)
    def _():
        sent(sums, 63 * MSG, fs_sem)
        sent(gsend, 63 * MSG, bs_sem)
        sent(crecv, 63, cs_sem)

    @pl.when(jnp.logical_not(is_home))
    def _():
        sent(sums, 64 * MSG, fs_sem)
        sent(gsend, 64 * MSG, bs_sem)
        sent(crecv, 64, cs_sem)

    sent(rs, 15, ar_send.at[0])
    sent(bb, 15, ar_send.at[1])
    sent(zr, 7, ar_send.at[2])
    sent(bz, 7, ar_send.at[3])
    sent(rs, 15, ar_send.at[4])


def shards(features, w_self, w_neigh, bias_vector, upstream, sources, edge_slots, mirror_rows):
    vmem = pl.BlockSpec(memory_space=pltpu.VMEM)
    scratch = [
        pltpu.VMEM((1, 4096), jnp.int32),
        pltpu.VMEM((1, 4096), jnp.int32),
        pltpu.VMEM((1024, 256), BF),
        pltpu.VMEM((4, 1024, CHUNK), F8),
        pltpu.VMEM((4, 1024, BLOCK), BF),
        pltpu.VMEM((1024, 256), BF),
        pltpu.VMEM((8, 1, 128), F32),
        pltpu.VMEM((1024, 256), BF),
        pltpu.VMEM((64, 1, 128), F32),
        pltpu.VMEM((4, BLOCK, 1024), BF),
        pltpu.VMEM((4, 1024, BLOCK), BF),
        pltpu.VMEM((1024, 256), F32),
        pltpu.VMEM((512, 256), F32),
        pltpu.VMEM((1024, 128), F32),
        pltpu.VMEM((512, 128), F32),
        pltpu.VMEM((1024, 256), BF),
        pltpu.VMEM((1024, 256), BF),
        pltpu.VMEM((1024, 256), BF),
        pltpu.VMEM((1024, 256), F32),
        pltpu.VMEM((512, 256), F32),
        pltpu.VMEM((512, 256), F32),
        pltpu.VMEM((2, 256, 256), F32),
        pltpu.VMEM((256, 256), F32),
        pltpu.VMEM((16, 16, 256), F32),
        pltpu.VMEM((8, 16, 256), F32),
        pltpu.VMEM((2, 16, 16, 256), F32),
        pltpu.VMEM((16, 1, 256), F32),
        pltpu.VMEM((8, 1, 256), F32),
        pltpu.VMEM((2, 1, 256), F32),
        pltpu.SemaphoreType.DMA((10,)),
        pltpu.SemaphoreType.DMA((10,)),
        pltpu.SemaphoreType.DMA,
        pltpu.SemaphoreType.DMA((4,)),
        pltpu.SemaphoreType.DMA,
        pltpu.SemaphoreType.DMA,
        pltpu.SemaphoreType.DMA,
        pltpu.SemaphoreType.DMA((4,)),
        pltpu.SemaphoreType.DMA((5,)),
        pltpu.SemaphoreType.DMA((5,)),
    ]
    hidden, igrad, gself, gneigh, gbias = pl.pallas_call(
        kernel,
        out_shape=(
            jax.ShapeDtypeStruct((512, 256), BF),
            jax.ShapeDtypeStruct((512, 256), BF),
            jax.ShapeDtypeStruct((256, 256), F32),
            jax.ShapeDtypeStruct((256, 256), F32),
            jax.ShapeDtypeStruct((1, 256), F32),
        ),
        in_specs=[vmem] * 8,
        out_specs=(vmem,) * 5,
        scratch_shapes=scratch,
        compiler_params=pltpu.CompilerParams(
            collective_id=0, has_side_effects=True, vmem_limit_bytes=48 * 2**20
        ),
        name="sage_layer",
    )(
        features, w_self, w_neigh, bias_vector.reshape(1, -1), upstream,
        sources.reshape(1, -1), edge_slots.reshape(1, -1), mirror_rows[0],
    )
    return hidden, igrad, gself, gneigh, gbias.reshape(-1)


def solution(mesh):
    in_specs = (
        P(("dom", "rep"), None),
        P(),
        P(),
        P(),
        P(("dom", "rep"), None),
        P(("dom", "rep")),
        P(("dom", "rep")),
        P("dom", None, None),
    )
    out_specs = (P(("dom", "rep"), None), P(("dom", "rep"), None), P(), P(), P())
    return jax.shard_map(shards, mesh=mesh, in_specs=in_specs, out_specs=out_specs, check_vma=False)
```

```python
import functools
import math

import jax
import jax.numpy as jnp
from jax import lax
from jax.experimental import pallas as pl
from jax.experimental.pallas import tpu as pltpu
from jax.sharding import PartitionSpec as P

MESH = pl.DeviceIdType.MESH
BF = jnp.bfloat16
F32 = jnp.float32
F8 = jnp.float8_e4m3fn

NN = (((1,), (0,)), ((), ()))
NT = (((1,), (1,)), ((), ()))
TN = (((0,), (0,)), ((), ()))

CHUNK = 2048
BLOCK = 256
MSG = 16


def dot(a, b, dims=NN):
    return lax.dot_general(a, b, dims, preferred_element_type=F32)


def one_hot_cols(index_row, count, dtype):
    n = index_row.shape[1]
    rows = lax.broadcasted_iota(jnp.int32, (count, n), 0).astype(jnp.int16)
    wanted = jnp.broadcast_to(index_row, (count, n)).astype(jnp.int16)
    return jnp.where(rows == wanted, jnp.ones((), BF), jnp.zeros((), BF)).astype(dtype)


def rows_at(start, count, unit):
    return pl.ds(pl.multiple_of(start, unit), count)


def kernel(
    feat_h, w_self_h, w_neigh_h, bias_h, up_h, src_h, slot_h, mir_h,
    hidden, igrad, gself, gneigh, gbias,
    w_self, w_neigh, bias, up, src, slot, mir, mcol, col_ref,
    fall, ssrc, at, sums, cnt, recv_f, crecv,
    pt, pm, nsum, nrecv, dpart, drecv, mg, gsend, recv_b, esum, erecv, presf, mn, pg,
    term, trecv, rs, zr, ag, bb, bz, b2,
    in_sem, rep_send, rep_recv, fs_sem, fr_sem, cs_sem, cr_sem, bs_sem, br_sem,
    ar_send, ar_recv,
):
    p = lax.axis_index("dom")
    r = lax.axis_index("rep")
    o = 1 - r
    x, y, z = p // 32, (p // 8) % 4, p % 8
    h, a, b = x // 2, x % 2, y // 2
    m = x * 4 + y
    my_idx = (a * 4 + y) * 8 + z
    is_home = h == r
    own_rows = rows_at(r * 512, 512, 512)
    other_rows = rows_at(o * 512, 512, 512)

    bar = pltpu.get_barrier_semaphore()

    def tell(dom, rep):
        pl.semaphore_signal(bar, inc=1, device_id=(dom, rep), device_id_type=MESH)

    loads = [
        pltpu.make_async_copy(source, target, in_sem.at[n])
        for n, (source, target) in enumerate((
            (src_h, src.at[0]), (slot_h, slot.at[0]), (feat_h, fall.at[own_rows, :]),
            (mir_h, mir), (w_self_h, w_self), (bias_h, bias), (w_neigh_h, w_neigh), (up_h, up),
        ))
    ]
    for load in loads:
        load.start()

    tell(p, o)

    def tell_half(k, c):
        @pl.when(jnp.logical_not(jnp.logical_and(is_home, k == my_idx)))
        def _():
            tell(r * 64 + k, h)

        return c

    lax.fori_loop(0, 64, tell_half, 0)
    lax.fori_loop(1, 16, lambda k, c: (tell(((m + k) % 16) * 8 + z, r), c)[1], 0)
    lax.fori_loop(1, 8, lambda k, c: (tell(m * 8 + (z + k) % 8, r), c)[1], 0)

    def pick_sources(which):
        def step(c, carry):
            cols = rows_at(c * CHUNK, CHUNK, CHUNK)
            ssrc[which * 2 + c] = one_hot_cols(src[which, :, cols], 1024, F8)
            return carry

        lax.fori_loop(0, 2, step, 0)

    loads[0].wait()
    pick_sources(0)
    for load in loads[1:3]:
        load.wait()

    pl.semaphore_wait(bar, 87 - jnp.where(is_home, 1, 0))

    def to_other(source, target, n):
        return pltpu.make_async_remote_copy(
            source, target, rep_send.at[n], rep_recv.at[n],
            device_id=(p, o), device_id_type=MESH,
        )

    c_src = to_other(src.at[0], src.at[1], 0)
    c_slot = to_other(slot.at[0], slot.at[1], 1)
    c_feat = to_other(fall.at[own_rows, :], fall.at[own_rows, :], 2)
    c_src.start()
    c_slot.start()
    c_feat.start()
    c_src.wait_recv()
    pick_sources(1)
    c_slot.wait_recv()
    c_feat.wait_recv()

    def send_block(t, source, target, send_sem, recv_sem, counts):
        i, j = (a + t // 2) % 2, (b + t % 2) % 2

        def step(k, c):
            line = i * 4 + 2 * j + k // 8
            idx = line * 8 + (z + k) % 8
            here = rows_at(idx * MSG, MSG, MSG)
            there = rows_at(my_idx * MSG, MSG, MSG)
            is_self = jnp.logical_and(is_home, idx == my_idx)

            @pl.when(jnp.logical_not(is_self))
            def _():
                dev = (r * 64 + idx, h)
                if counts:
                    pltpu.make_async_remote_copy(
                        cnt.at[line], crecv.at[my_idx], cs_sem, cr_sem,
                        device_id=dev, device_id_type=MESH,
                    ).start()
                pltpu.make_async_remote_copy(
                    source.at[here, :], target.at[there, :], send_sem, recv_sem.at[t],
                    device_id=dev, device_id_type=MESH,
                ).start()

            @pl.when(is_self)
            def _():
                if counts:
                    pltpu.make_async_copy(cnt.at[line], crecv.at[my_idx], cr_sem).start()
                pltpu.make_async_copy(
                    source.at[here, :], target.at[there, :], recv_sem.at[t]
                ).start()

            return c

        lax.fori_loop(0, 16, step, 0)

    def block_of(t):
        return (a + t // 2) % 2 * 2 + (b + t % 2) % 2

    def wait_block(t, target, recv_sem):
        part = target.at[rows_at(block_of(t) * BLOCK, BLOCK, BLOCK), :]
        pltpu.make_async_copy(part, part, recv_sem.at[t]).wait()

    def count_block(t, carry):
        blk = block_of(t)
        base = r * 1024 + blk * BLOCK
        acc = None
        for c in range(4):
            lo = (c % 2) * CHUNK
            sel = one_hot_cols(slot[c // 2, :, lo:lo + CHUNK] - base, BLOCK, F8)
            d = dot(ssrc[c], sel, NT)
            acc = d if acc is None else acc + d
        counted = jnp.sum(acc, axis=0, keepdims=True)
        cnt[blk * 2] = counted[:, :128]
        cnt[blk * 2 + 1] = counted[:, 128:]
        table = acc.astype(BF)
        at[blk] = table
        sums[rows_at(blk * BLOCK, BLOCK, BLOCK), :] = dot(table, fall[...], TN).astype(BF)
        send_block(t, sums, recv_f, fs_sem, fr_sem, True)
        return carry

    lax.fori_loop(0, 4, count_block, 0)

    for load in loads[3:]:
        load.wait()

    mcol[...] = jnp.concatenate([mir[...].astype(F32)] * 8, axis=0).T
    spread = mcol[rows_at(r * 64, 64, 64), :]
    spread = jnp.broadcast_to(spread[:, None, :], (64, 16, 128)).reshape(1024, 128)
    lane = lax.broadcasted_iota(jnp.int32, (1024, 128), 1)
    sub = lax.broadcasted_iota(jnp.int32, (1024, 128), 0)
    col = jnp.sum(jnp.where(lane == sub % 16, spread, 0.0), axis=1, keepdims=True)
    col_ref[...] = jnp.broadcast_to(col, (1024, 128)).reshape(4, BLOCK, 128)

    def master_block(q, carry):
        part = col_ref[q]
        pm[q] = one_hot_cols(part.T[0:1].astype(jnp.int32), 1024, BF)
        pt[q] = pm[q].T
        return carry

    lax.fori_loop(0, 4, master_block, 0)

    nsum[...] = jnp.zeros_like(nsum)
    presf[...] = dot(fall[own_rows, :], w_self[...]) + bias[...]

    pltpu.make_async_copy(crecv, crecv, cr_sem).wait()
    got = crecv[...].reshape(64, 128)
    wide = jnp.broadcast_to(got[:, None, :], (64, 16, 128)).reshape(1024, 128)
    wide = jnp.where(lane == z * 16 + sub % 16, wide, 0.0)
    high = jnp.floor(wide * (1.0 / 256))
    split = jnp.concatenate([high, wide - high * 256.0], axis=1).astype(BF)
    both = sum(dot(pm[q], split[q * BLOCK:(q + 1) * BLOCK]) for q in range(4))
    dpart[...] = both[:, :128] * 256.0 + both[:, 128:]
    c_deg = to_other(dpart.at[other_rows, :], drecv, 3)
    c_deg.start()

    c_sum = to_other(nsum.at[other_rows, :], nrecv, 4)

    def place_block(t, carry):
        blk = block_of(t)
        wait_block(t, recv_f, fr_sem)
        part = recv_f[rows_at(blk * BLOCK, BLOCK, BLOCK), :]
        nsum[other_rows, :] += dot(pm[blk, other_rows, :], part)

        @pl.when(t == 3)
        def _():
            c_sum.start()

        nsum[own_rows, :] += dot(pm[blk, own_rows, :], part)
        return carry

    lax.fori_loop(0, 4, place_block, 0)

    c_deg.wait_recv()
    c_sum.wait_recv()

    def dense_block(q, carry):
        rows = rows_at(q * 128, 128, 128)
        mine = rows_at(r * 512 + q * 128, 128, 128)
        degree = jnp.sum(dpart[mine, :] + drecv[rows, :], axis=1, keepdims=True)
        divisor = jnp.maximum(degree, 1.0)
        mean = ((nsum[mine, :] + nrecv[rows, :]) / divisor).astype(BF)
        pre = presf[rows, :] + dot(mean, w_neigh[...])
        gate = jax.nn.sigmoid(pre)
        pre_grad = up[rows, :].astype(F32) * (gate + pre * gate * (1.0 - gate))
        pre_grad = pre_grad.astype(BF)
        mg[mine, :] = (dot(pre_grad, w_neigh[...], NT) / divisor).astype(BF)
        hidden[rows, :] = (pre * gate).astype(BF)
        mn[rows, :] = mean
        pg[rows, :] = pre_grad
        return carry

    lax.fori_loop(0, 4, dense_block, 0)
    c_mg = to_other(mg.at[own_rows, :], mg.at[own_rows, :], 5)
    c_mg.start()
    term[0] = dot(fall[own_rows, :], pg[...], TN)
    term[1] = dot(mn[...], pg[...], TN)
    c_term = to_other(term.at[o], trecv, 6)
    c_term.start()
    bb[m] = jnp.sum(pg[...].astype(F32), axis=0, keepdims=True)

    def spread_to(peers, of, source, target, n):
        def step(k, c):
            pltpu.make_async_remote_copy(
                source(k), target, ar_send.at[n], ar_recv.at[n],
                device_id=(of(k), r), device_id_type=MESH,
            ).start()
            return c

        lax.fori_loop(1, peers, step, 0)

    def plane(k):
        return ((m + k) % 16) * 8 + z

    def line(k):
        return m * 8 + (z + k) % 8

    def wait_all(ref, count, sem):
        part = ref.at[pl.ds(0, count)]
        pltpu.make_async_copy(part, part, sem).wait()

    scale = 1.0 / math.sqrt(131072)
    tsum = term.at[r]
    c_bias = to_other(b2.at[r], b2.at[r], 7)
    c_ag = to_other(ag.at[r], ag.at[r], 8)

    def reduce_plane():
        c_term.wait_recv()
        tsum[...] += trecv[...]
        spread_to(
            16, plane,
            lambda k: tsum.at[rows_at(((m + k) % 16) * 16, 16, 16), :], rs.at[m], 0,
        )
        spread_to(16, plane, lambda k: bb.at[m], bb.at[m], 1)
        rs[m] = tsum[rows_at(m * 16, 16, 16), :]

    def reduce_line():
        wait_all(rs, 15, ar_recv.at[0])
        wait_all(bb, 15, ar_recv.at[1])
        zr[z] = jnp.sum(rs[...], axis=0)
        bz[z] = jnp.sum(bb[...], axis=0)
        spread_to(8, line, lambda k: zr.at[z], zr.at[z], 2)
        spread_to(8, line, lambda k: bz.at[z], bz.at[z], 3)

    def gather_plane():
        wait_all(zr, 7, ar_recv.at[2])
        wait_all(bz, 7, ar_recv.at[3])
        ag[r, m] = jnp.sum(zr[...], axis=0) * scale
        b2[r] = jnp.sum(bz[...], axis=0)
        spread_to(16, plane, lambda k: ag.at[r, m], ag.at[r, m], 4)
        c_bias.start()

    def gather_cores():
        wait_all(ag.at[r], 15, ar_recv.at[4])
        c_ag.start()

    c_mg.wait_recv()

    def return_block(t, carry):
        blk = block_of(t)
        here = rows_at(blk * BLOCK, BLOCK, BLOCK)
        gsend[here, :] = dot(pt[blk], mg[...]).astype(BF)
        send_block(t, gsend, recv_b, bs_sem, br_sem, False)

        @pl.when(t == 0)
        def _():
            reduce_plane()

        return carry

    lax.fori_loop(0, 4, return_block, 0)

    esum[own_rows, :] = dot(pg[...], w_self[...], NT)
    esum[other_rows, :] = jnp.zeros((512, 256), F32)
    c_edge = to_other(esum.at[other_rows, :], erecv, 9)

    def edge_block(t, carry):
        blk = block_of(t)

        @pl.when(t == 0)
        def _():
            reduce_line()

        @pl.when(t == 1)
        def _():
            gather_plane()

        @pl.when(t == 3)
        def _():
            gather_cores()

        wait_block(t, recv_b, br_sem)
        part = recv_b[rows_at(blk * BLOCK, BLOCK, BLOCK), :]
        esum[other_rows, :] += dot(at[blk, other_rows, :], part)

        @pl.when(t == 3)
        def _():
            c_edge.start()

        esum[own_rows, :] += dot(at[blk, own_rows, :], part)
        return carry

    lax.fori_loop(0, 4, edge_block, 0)

    c_bias.wait_recv()
    c_ag.wait_recv()
    gself[...] = ag[0].reshape(256, 256)
    gneigh[...] = ag[1].reshape(256, 256)
    gbias[...] = (b2[0] + b2[1]) * scale
    c_edge.wait_recv()
    igrad[...] = (esum[own_rows, :] + erecv[...]).astype(BF)

    for copy in (c_src, c_slot, c_feat, c_deg, c_sum, c_mg, c_term, c_bias, c_ag, c_edge):
        copy.wait_send()

    def sent(ref, count, sem):
        part = ref.at[pl.ds(0, count)]
        pltpu.make_async_copy(part, part, sem).wait()

    @pl.when(is_home)
    def _():
        sent(sums, 63 * MSG, fs_sem)
        sent(gsend, 63 * MSG, bs_sem)
        sent(crecv, 63, cs_sem)

    @pl.when(jnp.logical_not(is_home))
    def _():
        sent(sums, 64 * MSG, fs_sem)
        sent(gsend, 64 * MSG, bs_sem)
        sent(crecv, 64, cs_sem)

    sent(rs, 15, ar_send.at[0])
    sent(bb, 15, ar_send.at[1])
    sent(zr, 7, ar_send.at[2])
    sent(bz, 7, ar_send.at[3])
    sent(rs, 15, ar_send.at[4])


def write_out(*refs):
    n = len(refs) // 2
    sems = refs[-1]
    copies = [pltpu.make_async_copy(refs[i], refs[n + i], sems.at[i]) for i in range(n)]
    for copy in copies:
        copy.start()
    for copy in copies:
        copy.wait()


def shards(features, w_self, w_neigh, bias_vector, upstream, sources, edge_slots, mirror_rows):
    vmem = pl.BlockSpec(memory_space=pltpu.VMEM)
    hbm = pl.BlockSpec(memory_space=pltpu.HBM)
    scratch = [
        pltpu.VMEM((256, 256), BF),
        pltpu.VMEM((256, 256), BF),
        pltpu.VMEM((1, 256), F32),
        pltpu.VMEM((512, 256), BF),
        pltpu.VMEM((2, 1, 4096), jnp.int32),
        pltpu.VMEM((2, 1, 4096), jnp.int32),
        pltpu.VMEM((16, 128), jnp.int32),
        pltpu.VMEM((128, 128), F32),
        pltpu.VMEM((4, BLOCK, 128), F32),
        pltpu.VMEM((1024, 256), BF),
        pltpu.VMEM((4, 1024, CHUNK), F8),
        pltpu.VMEM((4, 1024, BLOCK), BF),
        pltpu.VMEM((1024, 256), BF),
        pltpu.VMEM((8, 1, 128), F32),
        pltpu.VMEM((1024, 256), BF),
        pltpu.VMEM((64, 1, 128), F32),
        pltpu.VMEM((4, BLOCK, 1024), BF),
        pltpu.VMEM((4, 1024, BLOCK), BF),
        pltpu.VMEM((1024, 256), F32),
        pltpu.VMEM((512, 256), F32),
        pltpu.VMEM((1024, 128), F32),
        pltpu.VMEM((512, 128), F32),
        pltpu.VMEM((1024, 256), BF),
        pltpu.VMEM((1024, 256), BF),
        pltpu.VMEM((1024, 256), BF),
        pltpu.VMEM((1024, 256), F32),
        pltpu.VMEM((512, 256), F32),
        pltpu.VMEM((512, 256), F32),
        pltpu.VMEM((512, 256), BF),
        pltpu.VMEM((512, 256), BF),
        pltpu.VMEM((2, 256, 256), F32),
        pltpu.VMEM((256, 256), F32),
        pltpu.VMEM((16, 16, 256), F32),
        pltpu.VMEM((8, 16, 256), F32),
        pltpu.VMEM((2, 16, 16, 256), F32),
        pltpu.VMEM((16, 1, 256), F32),
        pltpu.VMEM((8, 1, 256), F32),
        pltpu.VMEM((2, 1, 256), F32),
        pltpu.SemaphoreType.DMA((8,)),
        pltpu.SemaphoreType.DMA((10,)),
        pltpu.SemaphoreType.DMA((10,)),
        pltpu.SemaphoreType.DMA,
        pltpu.SemaphoreType.DMA((4,)),
        pltpu.SemaphoreType.DMA,
        pltpu.SemaphoreType.DMA,
        pltpu.SemaphoreType.DMA,
        pltpu.SemaphoreType.DMA((4,)),
        pltpu.SemaphoreType.DMA((5,)),
        pltpu.SemaphoreType.DMA((5,)),
    ]
    shapes = (
        jax.ShapeDtypeStruct((512, 256), BF),
        jax.ShapeDtypeStruct((512, 256), BF),
        jax.ShapeDtypeStruct((256, 256), F32),
        jax.ShapeDtypeStruct((256, 256), F32),
        jax.ShapeDtypeStruct((1, 256), F32),
    )
    results = pl.pallas_call(
        kernel,
        out_shape=shapes,
        in_specs=[hbm] * 8,
        out_specs=(vmem,) * 5,
        scratch_shapes=scratch,
        compiler_params=pltpu.CompilerParams(
            collective_id=0, has_side_effects=True, vmem_limit_bytes=63 * 2**20
        ),
        name="sage_layer",
    )(
        features, w_self, w_neigh, bias_vector.reshape(1, -1), upstream,
        sources.reshape(1, -1), edge_slots.reshape(1, -1), jnp.swapaxes(mirror_rows[0], 0, 1),
    )
    hidden, igrad, gself, gneigh, gbias = pl.pallas_call(
        write_out,
        out_shape=shapes,
        in_specs=[vmem] * 5,
        out_specs=(hbm,) * 5,
        scratch_shapes=[pltpu.SemaphoreType.DMA((5,))],
        name="write_out",
    )(*results)
    return hidden, igrad, gself, gneigh, gbias.reshape(-1)


def solution(mesh):
    in_specs = (
        P(("dom", "rep"), None),
        P(),
        P(),
        P(),
        P(("dom", "rep"), None),
        P(("dom", "rep")),
        P(("dom", "rep")),
        P("dom", None, None),
    )
    out_specs = (P(("dom", "rep"), None), P(("dom", "rep"), None), P(), P(), P())
    return jax.shard_map(shards, mesh=mesh, in_specs=in_specs, out_specs=out_specs, check_vma=False)
```

```python
import functools
import math

import jax
import jax.numpy as jnp
from jax import lax
from jax.experimental import pallas as pl
from jax.experimental.pallas import tpu as pltpu
from jax.sharding import PartitionSpec as P

MESH = pl.DeviceIdType.MESH
BF = jnp.bfloat16
F32 = jnp.float32
F8 = jnp.float8_e4m3fn

NN = (((1,), (0,)), ((), ()))
NT = (((1,), (1,)), ((), ()))
TN = (((0,), (0,)), ((), ()))

CHUNK = 2048
BLOCK = 256
MSG = 16
RT = BF
GT = BF
CT = BF
AT = (0, 1, 2, 6)


def dot(a, b, dims=NN):
    return lax.dot_general(a, b, dims, preferred_element_type=F32)


def one_hot_cols(index_row, count, dtype):
    n = index_row.shape[1]
    rows = lax.broadcasted_iota(jnp.int32, (count, n), 0).astype(jnp.int16)
    wanted = jnp.broadcast_to(index_row, (count, n)).astype(jnp.int16)
    return jnp.where(rows == wanted, jnp.ones((), BF), jnp.zeros((), BF)).astype(dtype)


def rows_at(start, count, unit):
    return pl.ds(pl.multiple_of(start, unit), count)


def kernel(
    feat_h, w_self_h, w_neigh_h, bias_h, up_h, src_h, slot_h, mir_h,
    hidden_h, igrad_h, gself_h, gneigh_h, gbias_h,
    hidden, igrad, gself, gneigh, gbias,
    w_self, w_neigh, bias, up, src, slot, mir, mcol, col_ref,
    fall, ssrc, at, sums, cnt, recv_f, crecv,
    pt, pm, nsum, nsend, nrecv, dacc, dpart, drecv, mg, gsend, recv_b, esum, esend, erecv, presf, mn, pg,
    term, trecv, tsum, rs, zr, ag, bb, bz, b2,
    in_sem, out_sem, rep_send, rep_recv, fs_sem, fr_sem, cs_sem, cr_sem, bs_sem, br_sem,
    ar_send, ar_recv,
):
    p = lax.axis_index("dom")
    r = lax.axis_index("rep")
    o = 1 - r
    x, y, z = p // 32, (p // 8) % 4, p % 8
    h, a, b = x // 2, x % 2, y // 2
    m = x * 4 + y
    my_idx = (a * 4 + y) * 8 + z
    is_home = h == r
    own_rows = rows_at(r * 512, 512, 512)
    other_rows = rows_at(o * 512, 512, 512)

    bar = pltpu.get_barrier_semaphore()

    def tell(dom, rep):
        pl.semaphore_signal(bar, inc=1, device_id=(dom, rep), device_id_type=MESH)

    loads = [
        pltpu.make_async_copy(source, target, in_sem.at[n])
        for n, (source, target) in enumerate((
            (src_h, src.at[0]), (slot_h, slot.at[0]), (feat_h, fall.at[own_rows, :]),
            (mir_h, mir), (w_self_h, w_self), (bias_h, bias), (w_neigh_h, w_neigh), (up_h, up),
        ))
    ]
    for load in loads:
        load.start()
    stores = [
        pltpu.make_async_copy(source, target, out_sem.at[n])
        for n, (source, target) in enumerate((
            (hidden, hidden_h), (igrad, igrad_h), (gself, gself_h), (gneigh, gneigh_h), (gbias, gbias_h),
        ))
    ]

    tell(p, o)

    def tell_half(k, c):
        @pl.when(jnp.logical_not(jnp.logical_and(is_home, k == my_idx)))
        def _():
            tell(r * 64 + k, h)

        return c

    lax.fori_loop(0, 64, tell_half, 0)
    lax.fori_loop(1, 16, lambda k, c: (tell(((m + k) % 16) * 8 + z, r), c)[1], 0)
    lax.fori_loop(1, 8, lambda k, c: (tell(m * 8 + (z + k) % 8, r), c)[1], 0)

    def pick_sources(which):
        def step(c, carry):
            cols = rows_at(c * CHUNK, CHUNK, CHUNK)
            ssrc[which * 2 + c] = one_hot_cols(src[which, :, cols], 1024, F8)
            return carry

        lax.fori_loop(0, 2, step, 0)

    loads[0].wait()
    pick_sources(0)
    for load in loads[1:3]:
        load.wait()

    pl.semaphore_wait(bar, 87 - jnp.where(is_home, 1, 0))

    def to_other(source, target, n):
        return pltpu.make_async_remote_copy(
            source, target, rep_send.at[n], rep_recv.at[n],
            device_id=(p, o), device_id_type=MESH,
        )

    c_src = to_other(src.at[0], src.at[1], 0)
    c_slot = to_other(slot.at[0], slot.at[1], 1)
    c_feat = to_other(fall.at[own_rows, :], fall.at[own_rows, :], 2)
    c_src.start()
    c_slot.start()
    c_feat.start()
    c_src.wait_recv()
    pick_sources(1)
    c_slot.wait_recv()
    c_feat.wait_recv()

    def send_block(t, source, target, send_sem, recv_sem, counts):
        i, j = (a + t // 2) % 2, (b + t % 2) % 2

        def step(k, c):
            line = i * 4 + 2 * j + k // 8
            idx = line * 8 + (z + k) % 8
            here = rows_at(idx * MSG, MSG, MSG)
            there = rows_at(my_idx * MSG, MSG, MSG)
            is_self = jnp.logical_and(is_home, idx == my_idx)

            @pl.when(jnp.logical_not(is_self))
            def _():
                dev = (r * 64 + idx, h)
                if counts:
                    pltpu.make_async_remote_copy(
                        cnt.at[line], crecv.at[my_idx], cs_sem, cr_sem.at[t],
                        device_id=dev, device_id_type=MESH,
                    ).start()
                pltpu.make_async_remote_copy(
                    source.at[here, :], target.at[there, :], send_sem, recv_sem.at[t],
                    device_id=dev, device_id_type=MESH,
                ).start()

            @pl.when(is_self)
            def _():
                if counts:
                    pltpu.make_async_copy(cnt.at[line], crecv.at[my_idx], cr_sem.at[t]).start()
                pltpu.make_async_copy(
                    source.at[here, :], target.at[there, :], recv_sem.at[t]
                ).start()

            return c

        lax.fori_loop(0, 16, step, 0)

    def block_of(t):
        return (a + t // 2) % 2 * 2 + (b + t % 2) % 2

    def wait_block(t, target, recv_sem):
        part = target.at[rows_at(block_of(t) * BLOCK, BLOCK, BLOCK), :]
        pltpu.make_async_copy(part, part, recv_sem.at[t]).wait()

    def count_block(t, carry):
        blk = block_of(t)
        base = r * 1024 + blk * BLOCK
        acc = None
        for c in range(4):
            lo = (c % 2) * CHUNK
            sel = one_hot_cols(slot[c // 2, :, lo:lo + CHUNK] - base, BLOCK, F8)
            d = dot(ssrc[c], sel, NT)
            acc = d if acc is None else acc + d
        counted = jnp.sum(acc, axis=0, keepdims=True)
        cnt[blk * 2] = counted[:, :128]
        cnt[blk * 2 + 1] = counted[:, 128:]
        table = acc.astype(BF)
        at[blk] = table
        sums[rows_at(blk * BLOCK, BLOCK, BLOCK), :] = dot(table, fall[...], TN).astype(BF)
        send_block(t, sums, recv_f, fs_sem, fr_sem, True)
        return carry

    lax.fori_loop(0, 4, count_block, 0)

    for load in loads[3:]:
        load.wait()

    mcol[...] = jnp.concatenate([mir[...].astype(F32)] * 8, axis=0).T
    spread = mcol[rows_at(r * 64, 64, 64), :]
    spread = jnp.broadcast_to(spread[:, None, :], (64, 16, 128)).reshape(1024, 128)
    lane = lax.broadcasted_iota(jnp.int32, (1024, 128), 1)
    sub = lax.broadcasted_iota(jnp.int32, (1024, 128), 0)
    col = jnp.sum(jnp.where(lane == sub % 16, spread, 0.0), axis=1, keepdims=True)
    col_ref[...] = jnp.broadcast_to(col, (1024, 128)).reshape(4, BLOCK, 128)

    def master_block(q, carry):
        part = col_ref[q]
        pm[q] = one_hot_cols(part.T[0:1].astype(jnp.int32), 1024, BF)
        pt[q] = pm[q].T
        return carry

    lax.fori_loop(0, 4, master_block, 0)

    nsum[...] = jnp.zeros_like(nsum)
    presf[...] = dot(fall[own_rows, :], w_self[...]) + bias[...]

    dacc[...] = jnp.zeros_like(dacc)

    c_sum = to_other(nsend, nrecv, 4)
    c_deg = to_other(dpart, drecv, 3)

    def place_block(t, carry):
        blk = block_of(t)
        places = pl.ds(pl.multiple_of(blk * 16, 16), 16)
        pltpu.make_async_copy(crecv.at[places], crecv.at[places], cr_sem.at[t]).wait()
        got = crecv[places].reshape(16, 128)
        wide = jnp.broadcast_to(got[:, None, :], (16, 16, 128)).reshape(BLOCK, 128)
        lane = lax.broadcasted_iota(jnp.int32, (BLOCK, 128), 1)
        sub = lax.broadcasted_iota(jnp.int32, (BLOCK, 128), 0)
        wide = jnp.where(lane == z * 16 + sub % 16, wide, 0.0)
        high = jnp.floor(wide * (1.0 / 256))
        split = jnp.concatenate([high, wide - high * 256.0], axis=1).astype(BF)
        dacc[other_rows, :] += dot(pm[blk, other_rows, :], split)
        dacc[own_rows, :] += dot(pm[blk, own_rows, :], split)

        @pl.when(t == 3)
        def _():
            dpart[...] = dacc[other_rows, :128] * 256.0 + dacc[other_rows, 128:]
            c_deg.start()

        wait_block(t, recv_f, fr_sem)
        part = recv_f[rows_at(blk * BLOCK, BLOCK, BLOCK), :]
        nsum[other_rows, :] += dot(pm[blk, other_rows, :], part)

        @pl.when(t == 3)
        def _():
            nsend[...] = nsum[other_rows, :].astype(CT)
            c_sum.start()

        nsum[own_rows, :] += dot(pm[blk, own_rows, :], part)
        return carry

    lax.fori_loop(0, 4, place_block, 0)
    dacc[own_rows, :128] = dacc[own_rows, :128] * 256.0 + dacc[own_rows, 128:]

    c_deg.wait_recv()
    c_sum.wait_recv()

    def dense_block(q, carry):
        rows = rows_at(q * 128, 128, 128)
        mine = rows_at(r * 512 + q * 128, 128, 128)
        degree = jnp.sum(dacc[mine, :128] + drecv[rows, :], axis=1, keepdims=True)
        divisor = jnp.maximum(degree, 1.0)
        mean = ((nsum[mine, :] + nrecv[rows, :]) / divisor).astype(BF)
        pre = presf[rows, :] + dot(mean, w_neigh[...])
        gate = jax.nn.sigmoid(pre)
        pre_grad = up[rows, :].astype(F32) * (gate + pre * gate * (1.0 - gate))
        pre_grad = pre_grad.astype(BF)
        mg[mine, :] = (dot(pre_grad, w_neigh[...], NT) / divisor).astype(BF)
        hidden[rows, :] = (pre * gate).astype(BF)
        mn[rows, :] = mean
        pg[rows, :] = pre_grad
        return carry

    lax.fori_loop(0, 4, dense_block, 0)
    stores[0].start()
    c_mg = to_other(mg.at[own_rows, :], mg.at[own_rows, :], 5)
    c_mg.start()
    term[0] = dot(fall[own_rows, :], pg[...], TN)
    term[1] = dot(mn[...], pg[...], TN)
    c_term = to_other(term.at[o], trecv, 6)
    c_term.start()
    bb[m] = jnp.sum(pg[...].astype(F32), axis=0, keepdims=True)

    def spread_to(peers, of, source, target, n):
        def step(k, c):
            pltpu.make_async_remote_copy(
                source(k), target, ar_send.at[n], ar_recv.at[n],
                device_id=(of(k), r), device_id_type=MESH,
            ).start()
            return c

        lax.fori_loop(1, peers, step, 0)

    def plane(k):
        return ((m + k) % 16) * 8 + z

    def line(k):
        return m * 8 + (z + k) % 8

    def wait_all(ref, count, sem):
        part = ref.at[pl.ds(0, count)]
        pltpu.make_async_copy(part, part, sem).wait()

    scale = 1.0 / math.sqrt(131072)
    c_bias = to_other(b2.at[r], b2.at[r], 7)
    c_ag = to_other(ag.at[r], ag.at[r], 8)

    def reduce_plane():
        c_term.wait_recv()
        tsum[...] = (term[r] + trecv[...]).astype(RT)
        spread_to(
            16, plane,
            lambda k: tsum.at[rows_at(((m + k) % 16) * 16, 16, 16), :], rs.at[m], 0,
        )
        spread_to(16, plane, lambda k: bb.at[m], bb.at[m], 1)
        rs[m] = tsum[rows_at(m * 16, 16, 16), :]

    def reduce_line():
        wait_all(rs, 15, ar_recv.at[0])
        wait_all(bb, 15, ar_recv.at[1])
        zr[z] = jnp.sum(rs[...].astype(F32), axis=0).astype(RT)
        bz[z] = jnp.sum(bb[...], axis=0)
        spread_to(8, line, lambda k: zr.at[z], zr.at[z], 2)
        spread_to(8, line, lambda k: bz.at[z], bz.at[z], 3)

    def gather_plane():
        wait_all(zr, 7, ar_recv.at[2])
        wait_all(bz, 7, ar_recv.at[3])
        ag[r, m] = (jnp.sum(zr[...].astype(F32), axis=0) * scale).astype(GT)
        b2[r] = jnp.sum(bz[...], axis=0)
        spread_to(16, plane, lambda k: ag.at[r, m], ag.at[r, m], 4)
        c_bias.start()

    def gather_cores():
        wait_all(ag.at[r], 15, ar_recv.at[4])
        c_ag.start()

    stages = (reduce_plane, reduce_line, gather_plane, gather_cores)

    def stages_at(t, first):
        for stage, when in zip(stages, AT):
            if first <= when < first + 4:
                pl.when(t == when - first)(stage)

    c_mg.wait_recv()

    def return_block(t, carry):
        blk = block_of(t)
        here = rows_at(blk * BLOCK, BLOCK, BLOCK)
        gsend[here, :] = dot(pt[blk], mg[...]).astype(BF)
        send_block(t, gsend, recv_b, bs_sem, br_sem, False)
        stages_at(t, 0)
        return carry

    if AT[0] < 0:
        reduce_plane()
    lax.fori_loop(0, 4, return_block, 0)

    esum[own_rows, :] = dot(pg[...], w_self[...], NT)
    esum[other_rows, :] = jnp.zeros((512, 256), F32)
    c_edge = to_other(esend, erecv, 9)

    def edge_block(t, carry):
        blk = block_of(t)

        stages_at(t, 4)
        wait_block(t, recv_b, br_sem)
        part = recv_b[rows_at(blk * BLOCK, BLOCK, BLOCK), :]
        esum[other_rows, :] += dot(at[blk, other_rows, :], part)

        @pl.when(t == 3)
        def _():
            esend[...] = esum[other_rows, :].astype(CT)
            c_edge.start()

        esum[own_rows, :] += dot(at[blk, own_rows, :], part)
        return carry

    lax.fori_loop(0, 4, edge_block, 0)

    def write_grads():
        c_bias.wait_recv()
        c_ag.wait_recv()
        gself[...] = ag[0].astype(F32).reshape(256, 256)
        gneigh[...] = ag[1].astype(F32).reshape(256, 256)
        gbias[...] = (b2[0] + b2[1]) * scale
        for store in stores[2:]:
            store.start()

    def write_input_grad():
        c_edge.wait_recv()
        igrad[...] = (esum[own_rows, :] + erecv[...]).astype(BF)
        stores[1].start()

    write_grads()
    write_input_grad()
    for store in stores:
        store.wait()

    for copy in (c_src, c_slot, c_feat, c_deg, c_sum, c_mg, c_term, c_bias, c_ag, c_edge):
        copy.wait_send()

    def sent(ref, count, sem):
        part = ref.at[pl.ds(0, count)]
        pltpu.make_async_copy(part, part, sem).wait()

    @pl.when(is_home)
    def _():
        sent(sums, 63 * MSG, fs_sem)
        sent(gsend, 63 * MSG, bs_sem)
        sent(crecv, 63, cs_sem)

    @pl.when(jnp.logical_not(is_home))
    def _():
        sent(sums, 64 * MSG, fs_sem)
        sent(gsend, 64 * MSG, bs_sem)
        sent(crecv, 64, cs_sem)

    sent(rs, 15, ar_send.at[0])
    sent(bb, 15, ar_send.at[1])
    sent(zr, 7, ar_send.at[2])
    sent(bz, 7, ar_send.at[3])
    sent(ag.at[0], 15, ar_send.at[4])


def write_out(*refs):
    n = len(refs) // 2
    sems = refs[-1]
    copies = [pltpu.make_async_copy(refs[i], refs[n + i], sems.at[i]) for i in range(n)]
    for copy in copies:
        copy.start()
    for copy in copies:
        copy.wait()


def shards(features, w_self, w_neigh, bias_vector, upstream, sources, edge_slots, mirror_rows):
    hbm = pl.BlockSpec(memory_space=pltpu.HBM)
    scratch = [
        pltpu.VMEM((512, 256), BF),
        pltpu.VMEM((512, 256), BF),
        pltpu.VMEM((256, 256), F32),
        pltpu.VMEM((256, 256), F32),
        pltpu.VMEM((1, 256), F32),
        pltpu.VMEM((256, 256), BF),
        pltpu.VMEM((256, 256), BF),
        pltpu.VMEM((1, 256), F32),
        pltpu.VMEM((512, 256), BF),
        pltpu.VMEM((2, 1, 4096), jnp.int32),
        pltpu.VMEM((2, 1, 4096), jnp.int32),
        pltpu.VMEM((16, 128), jnp.int32),
        pltpu.VMEM((128, 128), F32),
        pltpu.VMEM((4, BLOCK, 128), F32),
        pltpu.VMEM((1024, 256), BF),
        pltpu.VMEM((4, 1024, CHUNK), F8),
        pltpu.VMEM((4, 1024, BLOCK), BF),
        pltpu.VMEM((1024, 256), BF),
        pltpu.VMEM((8, 1, 128), F32),
        pltpu.VMEM((1024, 256), BF),
        pltpu.VMEM((64, 1, 128), F32),
        pltpu.VMEM((4, BLOCK, 1024), BF),
        pltpu.VMEM((4, 1024, BLOCK), BF),
        pltpu.VMEM((1024, 256), F32),
        pltpu.VMEM((512, 256), CT),
        pltpu.VMEM((512, 256), CT),
        pltpu.VMEM((1024, 256), F32),
        pltpu.VMEM((512, 128), F32),
        pltpu.VMEM((512, 128), F32),
        pltpu.VMEM((1024, 256), BF),
        pltpu.VMEM((1024, 256), BF),
        pltpu.VMEM((1024, 256), BF),
        pltpu.VMEM((1024, 256), F32),
        pltpu.VMEM((512, 256), CT),
        pltpu.VMEM((512, 256), CT),
        pltpu.VMEM((512, 256), F32),
        pltpu.VMEM((512, 256), BF),
        pltpu.VMEM((512, 256), BF),
        pltpu.VMEM((2, 256, 256), F32),
        pltpu.VMEM((256, 256), F32),
        pltpu.VMEM((256, 256), RT),
        pltpu.VMEM((16, 16, 256), RT),
        pltpu.VMEM((8, 16, 256), RT),
        pltpu.VMEM((2, 16, 16, 256), GT),
        pltpu.VMEM((16, 1, 256), F32),
        pltpu.VMEM((8, 1, 256), F32),
        pltpu.VMEM((2, 1, 256), F32),
        pltpu.SemaphoreType.DMA((8,)),
        pltpu.SemaphoreType.DMA((5,)),
        pltpu.SemaphoreType.DMA((10,)),
        pltpu.SemaphoreType.DMA((10,)),
        pltpu.SemaphoreType.DMA,
        pltpu.SemaphoreType.DMA((4,)),
        pltpu.SemaphoreType.DMA,
        pltpu.SemaphoreType.DMA((4,)),
        pltpu.SemaphoreType.DMA,
        pltpu.SemaphoreType.DMA((4,)),
        pltpu.SemaphoreType.DMA((5,)),
        pltpu.SemaphoreType.DMA((5,)),
    ]
    shapes = (
        jax.ShapeDtypeStruct((512, 256), BF),
        jax.ShapeDtypeStruct((512, 256), BF),
        jax.ShapeDtypeStruct((256, 256), F32),
        jax.ShapeDtypeStruct((256, 256), F32),
        jax.ShapeDtypeStruct((1, 256), F32),
    )
    results = pl.pallas_call(
        kernel,
        out_shape=shapes,
        in_specs=[hbm] * 8,
        out_specs=(hbm,) * 5,
        scratch_shapes=scratch,
        compiler_params=pltpu.CompilerParams(
            collective_id=0, has_side_effects=True, vmem_limit_bytes=63 * 2**20
        ),
        name="sage_layer",
    )(
        features, w_self, w_neigh, bias_vector.reshape(1, -1), upstream,
        sources.reshape(1, -1), edge_slots.reshape(1, -1), jnp.swapaxes(mirror_rows[0], 0, 1),
    )
    hidden, igrad, gself, gneigh, gbias = pl.pallas_call(
        write_out,
        out_shape=shapes,
        in_specs=[pl.BlockSpec(memory_space=pltpu.VMEM)] * 5,
        out_specs=(hbm,) * 5,
        scratch_shapes=[pltpu.SemaphoreType.DMA((5,))],
        name="write_out",
    )(*results)
    return hidden, igrad, gself, gneigh, gbias.reshape(-1)


def solution(mesh):
    in_specs = (
        P(("dom", "rep"), None),
        P(),
        P(),
        P(),
        P(("dom", "rep"), None),
        P(("dom", "rep")),
        P(("dom", "rep")),
        P("dom", None, None),
    )
    out_specs = (P(("dom", "rep"), None), P(("dom", "rep"), None), P(), P(), P())
    return jax.shard_map(shards, mesh=mesh, in_specs=in_specs, out_specs=out_specs, check_vma=False)
```

```python
import functools
import math

import jax
import jax.numpy as jnp
from jax import lax
from jax.experimental import pallas as pl
from jax.experimental.pallas import tpu as pltpu
from jax.sharding import PartitionSpec as P

MESH = pl.DeviceIdType.MESH
BF = jnp.bfloat16
F32 = jnp.float32
F8 = jnp.float8_e4m3fn

NN = (((1,), (0,)), ((), ()))
NT = (((1,), (1,)), ((), ()))
TN = (((0,), (0,)), ((), ()))

CHUNK = 2048
BLOCK = 256
MSG = 16
RT = BF
GT = BF
CT = BF
AT = (0, 1, 3, 6)


def dot(a, b, dims=NN):
    return lax.dot_general(a, b, dims, preferred_element_type=F32)


def one_hot_cols(index_row, count, dtype):
    n = index_row.shape[1]
    rows = lax.broadcasted_iota(jnp.int32, (count, n), 0).astype(jnp.int16)
    wanted = jnp.broadcast_to(index_row, (count, n)).astype(jnp.int16)
    return jnp.where(rows == wanted, jnp.ones((), BF), jnp.zeros((), BF)).astype(dtype)


def rows_at(start, count, unit):
    return pl.ds(pl.multiple_of(start, unit), count)


def kernel(
    feat_h, w_self_h, w_neigh_h, bias_h, up_h, src_h, slot_h, mir_h,
    hidden_h, igrad_h, gself_h, gneigh_h, gbias_h,
    hidden, igrad, gself, gneigh, gbias,
    w_self, w_neigh, bias, up, src, slot, mir, mcol, col_ref,
    fall, ssrc, at, sums, cnt, recv_f, crecv,
    pt, pm, nsum, nsend, nrecv, dacc, dpart, drecv, mg, gsend, recv_b, esum, esend, erecv, presf, mn, pg,
    term, trecv, tsum, rs, zr, ag, bb, bz, b2,
    in_sem, out_sem, rep_send, rep_recv, fs_sem, fr_sem, cs_sem, cr_sem, bs_sem, br_sem,
    ar_send, ar_recv,
):
    p = lax.axis_index("dom")
    r = lax.axis_index("rep")
    o = 1 - r
    x, y, z = p // 32, (p // 8) % 4, p % 8
    h, a, b = x // 2, x % 2, y // 2
    m = x * 4 + y
    my_idx = (a * 4 + y) * 8 + z
    is_home = h == r
    own_rows = rows_at(r * 512, 512, 512)
    other_rows = rows_at(o * 512, 512, 512)

    bar = pltpu.get_barrier_semaphore()

    def tell(dom, rep):
        pl.semaphore_signal(bar, inc=1, device_id=(dom, rep), device_id_type=MESH)

    loads = [
        pltpu.make_async_copy(source, target, in_sem.at[n])
        for n, (source, target) in enumerate((
            (src_h, src.at[0]), (slot_h, slot.at[0]), (feat_h, fall.at[own_rows, :]),
            (mir_h, mir), (w_self_h, w_self), (bias_h, bias), (w_neigh_h, w_neigh), (up_h, up),
        ))
    ]
    for load in loads:
        load.start()
    stores = [
        pltpu.make_async_copy(source, target, out_sem.at[n])
        for n, (source, target) in enumerate((
            (hidden, hidden_h), (igrad, igrad_h), (gself, gself_h), (gneigh, gneigh_h), (gbias, gbias_h),
        ))
    ]

    tell(p, o)

    def tell_half(k, c):
        @pl.when(jnp.logical_not(jnp.logical_and(is_home, k == my_idx)))
        def _():
            tell(r * 64 + k, h)

        return c

    lax.fori_loop(0, 64, tell_half, 0)
    lax.fori_loop(1, 16, lambda k, c: (tell(((m + k) % 16) * 8 + z, r), c)[1], 0)
    lax.fori_loop(1, 8, lambda k, c: (tell(m * 8 + (z + k) % 8, r), c)[1], 0)

    def pick_sources(which):
        def step(c, carry):
            cols = rows_at(c * CHUNK, CHUNK, CHUNK)
            ssrc[which * 2 + c] = one_hot_cols(src[which, :, cols], 1024, F8)
            return carry

        lax.fori_loop(0, 2, step, 0)

    loads[0].wait()
    pick_sources(0)
    for load in loads[1:3]:
        load.wait()

    pl.semaphore_wait(bar, 87 - jnp.where(is_home, 1, 0))

    def to_other(source, target, n):
        return pltpu.make_async_remote_copy(
            source, target, rep_send.at[n], rep_recv.at[n],
            device_id=(p, o), device_id_type=MESH,
        )

    c_src = to_other(src.at[0], src.at[1], 0)
    c_slot = to_other(slot.at[0], slot.at[1], 1)
    c_feat = to_other(fall.at[own_rows, :], fall.at[own_rows, :], 2)
    c_src.start()
    c_slot.start()
    c_feat.start()
    c_src.wait_recv()
    pick_sources(1)
    c_slot.wait_recv()
    c_feat.wait_recv()

    def send_block(t, source, target, send_sem, recv_sem, counts):
        i, j = (a + t // 2) % 2, (b + t % 2) % 2

        def step(k, c):
            line = i * 4 + 2 * j + k // 8
            idx = line * 8 + (z + k) % 8
            here = rows_at(idx * MSG, MSG, MSG)
            there = rows_at(my_idx * MSG, MSG, MSG)
            is_self = jnp.logical_and(is_home, idx == my_idx)

            @pl.when(jnp.logical_not(is_self))
            def _():
                dev = (r * 64 + idx, h)
                if counts:
                    pltpu.make_async_remote_copy(
                        cnt.at[line], crecv.at[my_idx], cs_sem, cr_sem.at[t],
                        device_id=dev, device_id_type=MESH,
                    ).start()
                pltpu.make_async_remote_copy(
                    source.at[here, :], target.at[there, :], send_sem, recv_sem.at[t],
                    device_id=dev, device_id_type=MESH,
                ).start()

            @pl.when(is_self)
            def _():
                if counts:
                    pltpu.make_async_copy(cnt.at[line], crecv.at[my_idx], cr_sem.at[t]).start()
                pltpu.make_async_copy(
                    source.at[here, :], target.at[there, :], recv_sem.at[t]
                ).start()

            return c

        lax.fori_loop(0, 16, step, 0)

    def block_of(t):
        return (a + t // 2) % 2 * 2 + (b + t % 2) % 2

    def wait_block(t, target, recv_sem):
        part = target.at[rows_at(block_of(t) * BLOCK, BLOCK, BLOCK), :]
        pltpu.make_async_copy(part, part, recv_sem.at[t]).wait()

    def count_block(t, carry):
        blk = block_of(t)
        base = r * 1024 + blk * BLOCK
        acc = None
        for c in range(4):
            lo = (c % 2) * CHUNK
            sel = one_hot_cols(slot[c // 2, :, lo:lo + CHUNK] - base, BLOCK, F8)
            d = dot(ssrc[c], sel, NT)
            acc = d if acc is None else acc + d
        counted = jnp.sum(acc, axis=0, keepdims=True)
        cnt[blk * 2] = counted[:, :128]
        cnt[blk * 2 + 1] = counted[:, 128:]
        table = acc.astype(BF)
        at[blk] = table
        sums[rows_at(blk * BLOCK, BLOCK, BLOCK), :] = dot(table, fall[...], TN).astype(BF)
        send_block(t, sums, recv_f, fs_sem, fr_sem, True)
        return carry

    lax.fori_loop(0, 4, count_block, 0)

    for load in loads[3:]:
        load.wait()

    mcol[...] = jnp.concatenate([mir[...].astype(F32)] * 8, axis=0).T
    spread = mcol[rows_at(r * 64, 64, 64), :]
    spread = jnp.broadcast_to(spread[:, None, :], (64, 16, 128)).reshape(1024, 128)
    lane = lax.broadcasted_iota(jnp.int32, (1024, 128), 1)
    sub = lax.broadcasted_iota(jnp.int32, (1024, 128), 0)
    col = jnp.sum(jnp.where(lane == sub % 16, spread, 0.0), axis=1, keepdims=True)
    col_ref[...] = jnp.broadcast_to(col, (1024, 128)).reshape(4, BLOCK, 128)

    def master_block(q, carry):
        part = col_ref[q]
        pm[q] = one_hot_cols(part.T[0:1].astype(jnp.int32), 1024, BF)
        pt[q] = pm[q].T
        return carry

    lax.fori_loop(0, 4, master_block, 0)

    nsum[...] = jnp.zeros_like(nsum)
    presf[...] = dot(fall[own_rows, :], w_self[...]) + bias[...]

    dacc[...] = jnp.zeros_like(dacc)

    c_sum = to_other(nsend, nrecv, 4)
    c_deg = to_other(dpart, drecv, 3)

    def place_block(t, carry):
        blk = block_of(t)
        places = pl.ds(pl.multiple_of(blk * 16, 16), 16)
        pltpu.make_async_copy(crecv.at[places], crecv.at[places], cr_sem.at[t]).wait()
        got = crecv[places].reshape(16, 128)
        wide = jnp.broadcast_to(got[:, None, :], (16, 16, 128)).reshape(BLOCK, 128)
        lane = lax.broadcasted_iota(jnp.int32, (BLOCK, 128), 1)
        sub = lax.broadcasted_iota(jnp.int32, (BLOCK, 128), 0)
        wide = jnp.where(lane == z * 16 + sub % 16, wide, 0.0)
        high = jnp.floor(wide * (1.0 / 256))
        split = jnp.concatenate([high, wide - high * 256.0], axis=1).astype(BF)
        dacc[other_rows, :] += dot(pm[blk, other_rows, :], split)
        dacc[own_rows, :] += dot(pm[blk, own_rows, :], split)

        @pl.when(t == 3)
        def _():
            dpart[...] = dacc[other_rows, :128] * 256.0 + dacc[other_rows, 128:]
            c_deg.start()

        wait_block(t, recv_f, fr_sem)
        part = recv_f[rows_at(blk * BLOCK, BLOCK, BLOCK), :]
        nsum[other_rows, :] += dot(pm[blk, other_rows, :], part)

        @pl.when(t == 3)
        def _():
            nsend[...] = nsum[other_rows, :].astype(CT)
            c_sum.start()

        nsum[own_rows, :] += dot(pm[blk, own_rows, :], part)
        return carry

    lax.fori_loop(0, 4, place_block, 0)
    dacc[own_rows, :128] = dacc[own_rows, :128] * 256.0 + dacc[own_rows, 128:]

    c_deg.wait_recv()
    c_sum.wait_recv()

    def dense_block(q, carry):
        rows = rows_at(q * 128, 128, 128)
        mine = rows_at(r * 512 + q * 128, 128, 128)
        degree = jnp.sum(dacc[mine, :128] + drecv[rows, :], axis=1, keepdims=True)
        divisor = jnp.maximum(degree, 1.0)
        mean = ((nsum[mine, :] + nrecv[rows, :]) / divisor).astype(BF)
        pre = presf[rows, :] + dot(mean, w_neigh[...])
        gate = jax.nn.sigmoid(pre)
        pre_grad = up[rows, :].astype(F32) * (gate + pre * gate * (1.0 - gate))
        pre_grad = pre_grad.astype(BF)
        mg[mine, :] = (dot(pre_grad, w_neigh[...], NT) / divisor).astype(BF)
        to_other(mg.at[mine, :], mg.at[mine, :], 5).start()
        hidden[rows, :] = (pre * gate).astype(BF)
        mn[rows, :] = mean
        pg[rows, :] = pre_grad
        return carry

    lax.fori_loop(0, 4, dense_block, 0)
    stores[0].start()
    c_mg = to_other(mg.at[own_rows, :], mg.at[own_rows, :], 5)
    term[0] = dot(fall[own_rows, :], pg[...], TN)
    term[1] = dot(mn[...], pg[...], TN)
    c_term = to_other(term.at[o], trecv, 6)
    c_term.start()
    bb[m] = jnp.sum(pg[...].astype(F32), axis=0, keepdims=True)

    def spread_to(peers, of, source, target, n):
        def step(k, c):
            pltpu.make_async_remote_copy(
                source(k), target, ar_send.at[n], ar_recv.at[n],
                device_id=(of(k), r), device_id_type=MESH,
            ).start()
            return c

        lax.fori_loop(1, peers, step, 0)

    def plane(k):
        return ((m + k) % 16) * 8 + z

    def line(k):
        return m * 8 + (z + k) % 8

    def wait_all(ref, count, sem):
        part = ref.at[pl.ds(0, count)]
        pltpu.make_async_copy(part, part, sem).wait()

    scale = 1.0 / math.sqrt(131072)
    c_bias = to_other(b2.at[r], b2.at[r], 7)
    c_ag = to_other(ag.at[r], ag.at[r], 8)

    def reduce_plane():
        c_term.wait_recv()
        tsum[...] = (term[r] + trecv[...]).astype(RT)
        spread_to(
            16, plane,
            lambda k: tsum.at[rows_at(((m + k) % 16) * 16, 16, 16), :], rs.at[m], 0,
        )
        spread_to(16, plane, lambda k: bb.at[m], bb.at[m], 1)
        rs[m] = tsum[rows_at(m * 16, 16, 16), :]

    def reduce_line():
        wait_all(rs, 15, ar_recv.at[0])
        wait_all(bb, 15, ar_recv.at[1])
        zr[z] = jnp.sum(rs[...].astype(F32), axis=0).astype(RT)
        bz[z] = jnp.sum(bb[...], axis=0)
        spread_to(8, line, lambda k: zr.at[z], zr.at[z], 2)
        spread_to(8, line, lambda k: bz.at[z], bz.at[z], 3)

    def gather_plane():
        wait_all(zr, 7, ar_recv.at[2])
        wait_all(bz, 7, ar_recv.at[3])
        ag[r, m] = (jnp.sum(zr[...].astype(F32), axis=0) * scale).astype(GT)
        b2[r] = jnp.sum(bz[...], axis=0)
        spread_to(16, plane, lambda k: ag.at[r, m], ag.at[r, m], 4)
        c_bias.start()

    def gather_cores():
        wait_all(ag.at[r], 15, ar_recv.at[4])
        c_ag.start()

    stages = (reduce_plane, reduce_line, gather_plane, gather_cores)

    def stages_at(t, first):
        for stage, when in zip(stages, AT):
            if first <= when < first + 4:
                pl.when(t == when - first)(stage)

    c_mg.wait_recv()

    def return_block(t, carry):
        blk = block_of(t)
        here = rows_at(blk * BLOCK, BLOCK, BLOCK)
        gsend[here, :] = dot(pt[blk], mg[...]).astype(BF)
        send_block(t, gsend, recv_b, bs_sem, br_sem, False)
        stages_at(t, 0)
        return carry

    if AT[0] < 0:
        reduce_plane()
    lax.fori_loop(0, 4, return_block, 0)

    esum[own_rows, :] = dot(pg[...], w_self[...], NT)
    esum[other_rows, :] = jnp.zeros((512, 256), F32)
    c_edge = to_other(esend, erecv, 9)

    def edge_block(t, carry):
        blk = block_of(t)

        stages_at(t, 4)
        wait_block(t, recv_b, br_sem)
        part = recv_b[rows_at(blk * BLOCK, BLOCK, BLOCK), :]
        esum[other_rows, :] += dot(at[blk, other_rows, :], part)

        @pl.when(t == 3)
        def _():
            esend[...] = esum[other_rows, :].astype(CT)
            c_edge.start()

        esum[own_rows, :] += dot(at[blk, own_rows, :], part)
        return carry

    lax.fori_loop(0, 4, edge_block, 0)

    def write_grads():
        c_bias.wait_recv()
        c_ag.wait_recv()
        gself[...] = ag[0].astype(F32).reshape(256, 256)
        gneigh[...] = ag[1].astype(F32).reshape(256, 256)
        gbias[...] = (b2[0] + b2[1]) * scale
        for store in stores[2:]:
            store.start()

    def write_input_grad():
        c_edge.wait_recv()
        igrad[...] = (esum[own_rows, :] + erecv[...]).astype(BF)
        stores[1].start()

    write_grads()
    write_input_grad()
    for store in stores:
        store.wait()

    for copy in (c_src, c_slot, c_feat, c_deg, c_sum, c_mg, c_term, c_bias, c_ag, c_edge):
        copy.wait_send()

    def sent(ref, count, sem):
        part = ref.at[pl.ds(0, count)]
        pltpu.make_async_copy(part, part, sem).wait()

    @pl.when(is_home)
    def _():
        sent(sums, 63 * MSG, fs_sem)
        sent(gsend, 63 * MSG, bs_sem)
        sent(crecv, 63, cs_sem)

    @pl.when(jnp.logical_not(is_home))
    def _():
        sent(sums, 64 * MSG, fs_sem)
        sent(gsend, 64 * MSG, bs_sem)
        sent(crecv, 64, cs_sem)

    sent(rs, 15, ar_send.at[0])
    sent(bb, 15, ar_send.at[1])
    sent(zr, 7, ar_send.at[2])
    sent(bz, 7, ar_send.at[3])
    sent(ag.at[0], 15, ar_send.at[4])


def write_out(*refs):
    n = len(refs) // 2
    sems = refs[-1]
    copies = [pltpu.make_async_copy(refs[i], refs[n + i], sems.at[i]) for i in range(n)]
    for copy in copies:
        copy.start()
    for copy in copies:
        copy.wait()


def shards(features, w_self, w_neigh, bias_vector, upstream, sources, edge_slots, mirror_rows):
    hbm = pl.BlockSpec(memory_space=pltpu.HBM)
    scratch = [
        pltpu.VMEM((512, 256), BF),
        pltpu.VMEM((512, 256), BF),
        pltpu.VMEM((256, 256), F32),
        pltpu.VMEM((256, 256), F32),
        pltpu.VMEM((1, 256), F32),
        pltpu.VMEM((256, 256), BF),
        pltpu.VMEM((256, 256), BF),
        pltpu.VMEM((1, 256), F32),
        pltpu.VMEM((512, 256), BF),
        pltpu.VMEM((2, 1, 4096), jnp.int32),
        pltpu.VMEM((2, 1, 4096), jnp.int32),
        pltpu.VMEM((16, 128), jnp.int32),
        pltpu.VMEM((128, 128), F32),
        pltpu.VMEM((4, BLOCK, 128), F32),
        pltpu.VMEM((1024, 256), BF),
        pltpu.VMEM((4, 1024, CHUNK), F8),
        pltpu.VMEM((4, 1024, BLOCK), BF),
        pltpu.VMEM((1024, 256), BF),
        pltpu.VMEM((8, 1, 128), F32),
        pltpu.VMEM((1024, 256), BF),
        pltpu.VMEM((64, 1, 128), F32),
        pltpu.VMEM((4, BLOCK, 1024), BF),
        pltpu.VMEM((4, 1024, BLOCK), BF),
        pltpu.VMEM((1024, 256), F32),
        pltpu.VMEM((512, 256), CT),
        pltpu.VMEM((512, 256), CT),
        pltpu.VMEM((1024, 256), F32),
        pltpu.VMEM((512, 128), F32),
        pltpu.VMEM((512, 128), F32),
        pltpu.VMEM((1024, 256), BF),
        pltpu.VMEM((1024, 256), BF),
        pltpu.VMEM((1024, 256), BF),
        pltpu.VMEM((1024, 256), F32),
        pltpu.VMEM((512, 256), CT),
        pltpu.VMEM((512, 256), CT),
        pltpu.VMEM((512, 256), F32),
        pltpu.VMEM((512, 256), BF),
        pltpu.VMEM((512, 256), BF),
        pltpu.VMEM((2, 256, 256), F32),
        pltpu.VMEM((256, 256), F32),
        pltpu.VMEM((256, 256), RT),
        pltpu.VMEM((16, 16, 256), RT),
        pltpu.VMEM((8, 16, 256), RT),
        pltpu.VMEM((2, 16, 16, 256), GT),
        pltpu.VMEM((16, 1, 256), F32),
        pltpu.VMEM((8, 1, 256), F32),
        pltpu.VMEM((2, 1, 256), F32),
        pltpu.SemaphoreType.DMA((8,)),
        pltpu.SemaphoreType.DMA((5,)),
        pltpu.SemaphoreType.DMA((10,)),
        pltpu.SemaphoreType.DMA((10,)),
        pltpu.SemaphoreType.DMA,
        pltpu.SemaphoreType.DMA((4,)),
        pltpu.SemaphoreType.DMA,
        pltpu.SemaphoreType.DMA((4,)),
        pltpu.SemaphoreType.DMA,
        pltpu.SemaphoreType.DMA((4,)),
        pltpu.SemaphoreType.DMA((5,)),
        pltpu.SemaphoreType.DMA((5,)),
    ]
    shapes = (
        jax.ShapeDtypeStruct((512, 256), BF),
        jax.ShapeDtypeStruct((512, 256), BF),
        jax.ShapeDtypeStruct((256, 256), F32),
        jax.ShapeDtypeStruct((256, 256), F32),
        jax.ShapeDtypeStruct((1, 256), F32),
    )
    results = pl.pallas_call(
        kernel,
        out_shape=shapes,
        in_specs=[hbm] * 8,
        out_specs=(hbm,) * 5,
        scratch_shapes=scratch,
        compiler_params=pltpu.CompilerParams(
            collective_id=0, has_side_effects=True, vmem_limit_bytes=63 * 2**20
        ),
        name="sage_layer",
    )(
        features, w_self, w_neigh, bias_vector.reshape(1, -1), upstream,
        sources.reshape(1, -1), edge_slots.reshape(1, -1), jnp.swapaxes(mirror_rows[0], 0, 1),
    )
    hidden, igrad, gself, gneigh, gbias = pl.pallas_call(
        write_out,
        out_shape=shapes,
        in_specs=[pl.BlockSpec(memory_space=pltpu.VMEM)] * 5,
        out_specs=(hbm,) * 5,
        scratch_shapes=[pltpu.SemaphoreType.DMA((5,))],
        name="write_out",
    )(*results)
    return hidden, igrad, gself, gneigh, gbias.reshape(-1)


def solution(mesh):
    in_specs = (
        P(("dom", "rep"), None),
        P(),
        P(),
        P(),
        P(("dom", "rep"), None),
        P(("dom", "rep")),
        P(("dom", "rep")),
        P("dom", None, None),
    )
    out_specs = (P(("dom", "rep"), None), P(("dom", "rep"), None), P(), P(), P())
    return jax.shard_map(shards, mesh=mesh, in_specs=in_specs, out_specs=out_specs, check_vma=False)
```
